32 devices in a mesh: groups: 2 (over y), rows: 4 (over z), cols: 4 (over x, core).
Axes of the slice: x: 2, y: 2, z: 4, core: 2. Of those that a mesh axis runs over, the one named last changes fastest.
Arguments:
- covariance: float32 [1024, 512], P(('groups', 'rows'), 'cols'), parts along dimension 0, as said below
- block_cols: int32 [8, 7], P(('groups', 'rows')), parts along dimension 0, may hold values from 0 to 3, as said below
- trans_blocks: float32 [8, 7, 128, 128], P(('groups', 'rows')), parts along dimension 0, may hold values from -0.1875 to 0.1875
- noise_pattern: int32 [8], P(('groups', 'rows')), parts along dimension 0, may hold values from 0 to 7
- noise_table: float32 [8, 128, 128], replicated, may hold values from -3 to 3
Outputs:
- forecast: float32 [1024, 512], P(('groups', 'rows'), 'cols'), parts along dimension 0
The draws below stay inside these ranges and needn't reach their ends.
There are 2 independent parts, one for each index of `groups`. The reference program is written for one: setup_inputs(seed, part) draws one part's arguments, and reference() takes and returns one part's arrays. A program takes and returns all parts, laid end to end along the dimension named above; an argument that names none is the same for every part. Nothing has to cross between parts.
Inputs may be any that keep to these rules, and one draw needn't show every extreme that they name: covariance is exactly symmetric. block_cols[i, 0] = i; for k >= 1, block_cols[i, k] = (i + o) mod 4 for 6 distinct nonzero offsets o between -4 and 4.
All inputs are finite; a program needn't handle non-finite values.
Results may differ from the reference program's by a relative error of at most 0.000096.
Values sent between devices are 32-bit elements; how exact they have to be, the bound alone decides.
A program may use at most 64 MiB of HBM per device.

```python
import jax
import jax.numpy as jnp
from jax import lax

BLK = 128
REACH = 4
NNZ = 7
NOISE_KINDS = 8
NB = 4
NW = 512


def draw_covariance(key, part):
    normal_draw = jax.random.normal(key, (NW, NW), jnp.float32)
    symmetric = (normal_draw + normal_draw.T) * 0.5
    return symmetric + 2.0 * jnp.eye(NW, dtype=jnp.float32)


def draw_block_cols(key, part):
    row_keys = jax.random.split(key, NB)
    nonzero = jnp.concatenate([jnp.arange(-REACH, 0, dtype=jnp.int32), jnp.arange(1, REACH + 1, dtype=jnp.int32)])

    def choose(row_key):
        return jax.random.permutation(row_key, nonzero)[:NNZ - 1]
    chosen = jax.vmap(choose)(row_keys)
    offsets = jnp.concatenate([jnp.zeros((NB, 1), jnp.int32), chosen], axis=1)
    return (jnp.arange(NB, dtype=jnp.int32)[:, None] + offsets) % NB


def with_ends(array, stream_key, low, high):
    longest = array.shape.index(max(array.shape))
    spots = []
    for shift in (0, 1):
        where = [jax.random.randint(jax.random.fold_in(stream_key, axis), (), 0, length) for axis, length in enumerate(array.shape)]
        where[longest] = (where[longest] + shift) % array.shape[longest]
        spots.append(tuple(where))
    return array.at[spots[0]].set(low).at[spots[1]].set(high)


def shard_levels(rng, shape, cuts, smallest, top_value):
    factor_of = 1.0
    for axis_at, shards_of in cuts:
        draws = jax.random.uniform(jax.random.fold_in(jax.random.fold_in(rng, 6), axis_at), (shards_of,), jnp.float32, smallest / len(cuts), top_value / len(cuts))
        factor_of = factor_of * jnp.repeat(jnp.exp(draws), shape[axis_at] // shards_of).reshape((-1,) + (1,) * (len(shape) - 1 - axis_at))
    return factor_of


def bell_draw(rng, shape, spread, most, pieces=(), held_as=jnp.bfloat16):
    values = spread * jax.random.normal(rng, shape, jnp.float32)
    if pieces:
        values = values * shard_levels(rng, shape, pieces, -0.22, 0.18)
    return jnp.clip(values, -most, most).astype(held_as)


def setup_inputs(seed: int = 0, part: int = 0) -> dict:
    keys = jax.random.split(jax.random.key(seed), 6)
    own_keys = jax.random.split(jax.random.fold_in(keys[5], part), 6)
    covariance = draw_covariance(jax.random.fold_in(jax.random.fold_in(keys[5], part), 71), part)
    block_cols = draw_block_cols(jax.random.fold_in(jax.random.fold_in(keys[5], part), 71), part)
    trans_blocks = bell_draw(own_keys[2], (NB, NNZ, BLK, BLK), (NNZ * BLK) ** -0.5, 0.1875, ((0, 4),), jnp.float32)
    noise_pattern = with_ends(jax.random.randint(own_keys[3], (NB,), 0, NOISE_KINDS), jax.random.fold_in(own_keys[3], 1), 0, NOISE_KINDS - 1).astype(jnp.int32)
    noise_table = bell_draw(keys[4], (NOISE_KINDS, BLK, BLK), 0.5, 3.0, (), jnp.float32)
    return {"covariance": covariance, "block_cols": block_cols, "trans_blocks": trans_blocks, "noise_pattern": noise_pattern, "noise_table": noise_table}


def propagate(matrix, block_cols, trans_blocks):
    row_blocks = matrix.reshape(NB, BLK, NW)

    def block_row(row_index):
        picked = jnp.take(row_blocks, block_cols[row_index], axis=0)
        return jnp.einsum("kab,kbn->an", trans_blocks[row_index], picked, precision=lax.Precision.HIGHEST)

    products = lax.map(block_row, jnp.arange(NB, dtype=jnp.int32))
    return products.reshape(NW, NW)


def noise_blocks(noise_pattern, noise_table):
    symmetric = (noise_table + jnp.transpose(noise_table, (0, 2, 1))) * 0.5
    onehot = (noise_pattern[:, None] == jnp.arange(NOISE_KINDS, dtype=jnp.int32)[None, :]).astype(jnp.float32)
    picked = jnp.dot(onehot, symmetric.reshape(NOISE_KINDS, BLK * BLK), precision=lax.Precision.HIGHEST, preferred_element_type=jnp.float32)
    return picked.reshape(-1, BLK, BLK)


def reference(covariance, block_cols, trans_blocks, noise_pattern, noise_table):
    propagated = propagate(covariance, block_cols, trans_blocks)
    carried = propagate(propagated.T, block_cols, trans_blocks).T
    blocks = carried.reshape(NB, BLK, NB, BLK)
    diagonal_index = jnp.arange(NB, dtype=jnp.int32)
    blocks = blocks.at[diagonal_index, :, diagonal_index, :].add(noise_blocks(noise_pattern, noise_table))
    return blocks.reshape(NW, NW)
```

```python
import functools

import jax
import jax.numpy as jnp
from jax import lax
from jax.experimental import pallas as pl
from jax.experimental.pallas import tpu as pltpu
from jax.sharding import PartitionSpec as P

REACH = 4
MESH = pl.DeviceIdType.MESH


def passed_along(value, axis, by):
    size = lax.axis_size(axis)
    return lax.ppermute(value, axis, [(i, (i + by) % size) for i in range(size)])


def neighbor_strips(local_tile, shards):
    lower_side = [None] * shards
    upper_side = [None] * shards
    for distance in list(range(-shards, 0)) + list(range(1, shards + 1)):
        incoming = passed_along(local_tile, "rows", -distance)
        if distance < 0:
            lower_side[shards + distance] = incoming
        else:
            upper_side[distance - 1] = incoming
    return (lower_side, upper_side)


def propagate_rows(local_tile, block_cols, trans_blocks):
    tile_height, tile_width = local_tile.shape
    blocks_here = block_cols.shape[0]
    block_size = trans_blocks.shape[2]
    total_blocks = blocks_here * lax.axis_size("rows")
    shards = -(-REACH // blocks_here)
    lower_side, upper_side = neighbor_strips(local_tile, shards)
    extended = jnp.concatenate(lower_side + [local_tile] + upper_side, axis=0)
    ext_blocks = extended.reshape(-1, block_size, tile_width)
    local_rows = jnp.arange(blocks_here, dtype=jnp.int32)
    first_block = lax.axis_index("rows") * blocks_here + local_rows
    offsets = (block_cols - first_block[:, None] + REACH) % total_blocks - REACH
    positions = shards * blocks_here + local_rows[:, None] + offsets
    result = jnp.zeros((blocks_here, block_size, tile_width), jnp.float32)
    for column_slot in range(block_cols.shape[1]):
        picked = jnp.take(ext_blocks, positions[:, column_slot], axis=0)
        result = result + jnp.einsum(
            "iab,ibw->iaw", trans_blocks[:, column_slot], picked, precision=lax.Precision.HIGHEST
        )
    return result.reshape(tile_height, tile_width)


def transpose_tile(local_tile):
    tile_height, tile_width = local_tile.shape
    col_count = lax.axis_size("cols")
    row_group = lax.axis_size("rows") // col_count
    quarter = tile_height // col_count
    section_one = lax.all_to_all(local_tile, "cols", split_axis=0, concat_axis=1, tiled=True)
    arrived = lax.all_to_all(
        lax.all_to_all(section_one, "rows", split_axis=1, concat_axis=0, tiled=True),
        "cols",
        split_axis=0,
        concat_axis=1,
        tiled=True,
    )
    pieces = arrived.reshape(row_group, quarter, col_count, tile_height)
    return jnp.transpose(pieces, (3, 0, 2, 1)).reshape(tile_height, tile_width)


def noise_tile(noise_pattern, noise_table, tile_height, tile_width):
    block_size = noise_table.shape[1]
    kinds = noise_table.shape[0]
    blocks_here = noise_pattern.shape[0]
    row_group = lax.axis_size("rows") // lax.axis_size("cols")
    row_index = lax.axis_index("rows")
    present = (row_index // row_group == lax.axis_index("cols")).astype(jnp.float32)
    symmetric = (noise_table + jnp.transpose(noise_table, (0, 2, 1))) * 0.5
    onehot = (noise_pattern[:, None] == jnp.arange(kinds, dtype=jnp.int32)[None, :]).astype(
        jnp.float32
    )
    picked = jnp.dot(
        onehot,
        symmetric.reshape(kinds, block_size * block_size),
        precision=lax.Precision.HIGHEST,
        preferred_element_type=jnp.float32,
    )
    picked = picked.reshape(blocks_here, block_size, block_size)
    identity = jnp.eye(blocks_here, dtype=jnp.float32)
    diagonal_tile = (picked[:, :, None, :] * identity[:, None, :, None]).reshape(
        tile_height, tile_height
    )
    start = row_index % row_group * tile_height
    placed = lax.dynamic_update_slice(
        jnp.zeros((tile_height, tile_width), jnp.float32), diagonal_tile, (jnp.int32(0), start)
    )
    return present * placed


def split(value):
    high = value.astype(jnp.bfloat16)
    return high, (value - high.astype(jnp.float32)).astype(jnp.bfloat16)


def product(left, right):
    left_high, left_low = left
    right_high, right_low = right
    dot = functools.partial(jnp.dot, preferred_element_type=jnp.float32)
    return dot(left_high, right_high) + (dot(left_high, right_low) + dot(left_low, right_high))


def square_kernel(
    size,
    cols_ref,
    pattern_ref,
    cov_ref,
    trans_ref,
    table_ref,
    out_ref,
    trans,
    table,
    own,
    rows_high,
    rows_low,
    turned_high,
    turned_low,
    tiles,
    sending,
    pieces,
    noise,
    local_sem,
    tile_send,
    tile_recv,
    piece_send,
    piece_recv,
):
    group = lax.axis_index("groups")
    row = lax.axis_index("rows")
    col = lax.axis_index("cols")
    diagonal = row == col

    get_cov = pltpu.make_async_copy(cov_ref, own, local_sem.at[0])
    get_trans = pltpu.make_async_copy(trans_ref, trans, local_sem.at[1])
    get_table = pltpu.make_async_copy(table_ref, table, local_sem.at[2])
    get_cov.start()
    get_trans.start()
    get_table.start()

    barrier = pltpu.get_barrier_semaphore()

    def greet(to_row, to_col):
        pl.semaphore_signal(
            barrier, inc=1, device_id=(group, to_row, to_col), device_id_type=MESH
        )

    for step in range(1, size):
        greet((row + step) % size, col)
        greet(col, (row + step) % size)

    @pl.when(jnp.logical_not(diagonal))
    def _():
        greet(col, row)

    get_cov.wait()
    sending[...] = own[...].T
    get_trans.wait()
    for j in range(size):
        block = jnp.zeros(own.shape, jnp.float32)
        for k in range(trans.shape[1]):
            block = block + jnp.where(cols_ref[0, k] == j, trans[0, k], 0.0)
        high, low = split(block)
        rows_high[j] = high
        rows_low[j] = low
        high, low = split(block.T)
        turned_high[j] = high
        turned_low[j] = low
    get_table.wait()
    noise[...] = jnp.zeros(noise.shape, jnp.float32)

    @pl.when(diagonal)
    def _():
        kind = table[pattern_ref[0]]
        noise[...] = (kind + kind.T) * 0.5

    @pl.when(diagonal)
    def _():
        pl.semaphore_wait(barrier, 2 * (size - 1))

    @pl.when(jnp.logical_not(diagonal))
    def _():
        pl.semaphore_wait(barrier, 2 * size - 1)

    tile_copies = []
    for step in range(1, size):
        tile_copies.append(
            pltpu.make_async_remote_copy(
                src_ref=sending,
                dst_ref=tiles.at[step - 1],
                send_sem=tile_send.at[step - 1],
                recv_sem=tile_recv.at[step - 1],
                device_id=(group, (row + step) % size, col),
                device_id_type=MESH,
            )
        )
        tile_copies[-1].start()

    total = product(split(sending[...]), (turned_high[row], turned_low[row]))
    for step in range(1, size):
        tile_copies[step - 1].wait_recv()
        source = (row + size - step) % size
        total = total + product(
            split(tiles[step - 1]), (turned_high[source], turned_low[source])
        )
    for copy in tile_copies:
        copy.wait_send()
    sending[...] = total

    def piece_copy(step):
        return pltpu.make_async_remote_copy(
            src_ref=sending,
            dst_ref=pieces.at[col],
            send_sem=piece_send.at[step],
            recv_sem=piece_recv.at[col],
            device_id=(group, (row + step) % size, row),
            device_id_type=MESH,
        )

    def arrival(source):
        return pltpu.make_async_remote_copy(
            src_ref=sending,
            dst_ref=pieces.at[source],
            send_sem=piece_send.at[0],
            recv_sem=piece_recv.at[source],
            device_id=(group, col, source),
            device_id_type=MESH,
        )

    for step in range(1, size):
        piece_copy(step).start()

    @pl.when(jnp.logical_not(diagonal))
    def _():
        piece_copy(0).start()

    @pl.when(diagonal)
    def _():
        pieces[col] = sending[...]

    result = noise[...]
    for step in range(size):
        source = (col + step) % size
        if step == 0:

            @pl.when(jnp.logical_not(diagonal))
            def _():
                arrival(source).wait_recv()
        else:
            arrival(source).wait_recv()
        result = result + product(
            (rows_high[source], rows_low[source]), split(pieces[source])
        )
    out_ref[...] = result

    for step in range(1, size):
        piece_copy(step).wait_send()

    @pl.when(jnp.logical_not(diagonal))
    def _():
        piece_copy(0).wait_send()


def square_body(covariance, block_cols, trans_blocks, noise_pattern, noise_table):
    size = lax.axis_size("rows")
    tile = covariance.shape
    copies = pltpu.SemaphoreType.DMA
    return pl.pallas_call(
        functools.partial(square_kernel, size),
        out_shape=jax.ShapeDtypeStruct(tile, jnp.float32),
        in_specs=[
            pl.BlockSpec(memory_space=pltpu.SMEM),
            pl.BlockSpec(memory_space=pltpu.SMEM),
            pl.BlockSpec(memory_space=pl.ANY),
            pl.BlockSpec(memory_space=pl.ANY),
            pl.BlockSpec(memory_space=pl.ANY),
        ],
        out_specs=pl.BlockSpec(memory_space=pltpu.VMEM),
        scratch_shapes=[
            pltpu.VMEM(trans_blocks.shape, jnp.float32),
            pltpu.VMEM(noise_table.shape, jnp.float32),
            pltpu.VMEM(tile, jnp.float32),
            pltpu.VMEM((size, *tile), jnp.bfloat16),
            pltpu.VMEM((size, *tile), jnp.bfloat16),
            pltpu.VMEM((size, *tile), jnp.bfloat16),
            pltpu.VMEM((size, *tile), jnp.bfloat16),
            pltpu.VMEM((size - 1, *tile), jnp.float32),
            pltpu.VMEM(tile, jnp.float32),
            pltpu.VMEM((size, *tile), jnp.float32),
            pltpu.VMEM(tile, jnp.float32),
            copies((3,)),
            copies((size - 1,)),
            copies((size - 1,)),
            copies((size,)),
            copies((size,)),
        ],
        compiler_params=pltpu.CompilerParams(collective_id=0, has_side_effects=True),
    )(block_cols, noise_pattern, covariance, trans_blocks, noise_table)


def body(covariance, block_cols, trans_blocks, noise_pattern, noise_table):
    tile_height, tile_width = covariance.shape
    propagated = propagate_rows(covariance, block_cols, trans_blocks)
    carried = propagate_rows(transpose_tile(propagated), block_cols, trans_blocks)
    return carried + noise_tile(noise_pattern, noise_table, tile_height, tile_width)


def device_body(covariance, block_cols, trans_blocks, noise_pattern, noise_table):
    block = trans_blocks.shape[2]
    square = lax.axis_size("rows") == lax.axis_size("cols")
    chosen = square_body if square and covariance.shape == (block, block) else body
    return chosen(covariance, block_cols, trans_blocks, noise_pattern, noise_table)


def solution(mesh):
    placed = (
        P(("groups", "rows"), "cols"),
        P(("groups", "rows"), None),
        P(("groups", "rows"), None, None, None),
        P(("groups", "rows")),
        P(),
    )
    return jax.shard_map(
        device_body, mesh=mesh, in_specs=placed, out_specs=P(("groups", "rows"), "cols"), check_vma=False
    )
```

```python
import functools

import jax
import jax.numpy as jnp
from jax import lax
from jax.experimental import pallas as pl
from jax.experimental.pallas import tpu as pltpu
from jax.sharding import PartitionSpec as P

REACH = 4
CHUNKS = 2
MESH = pl.DeviceIdType.MESH


def passed_along(value, axis, by):
    size = lax.axis_size(axis)
    return lax.ppermute(value, axis, [(i, (i + by) % size) for i in range(size)])


def neighbor_strips(local_tile, shards):
    lower_side = [None] * shards
    upper_side = [None] * shards
    for distance in list(range(-shards, 0)) + list(range(1, shards + 1)):
        incoming = passed_along(local_tile, "rows", -distance)
        if distance < 0:
            lower_side[shards + distance] = incoming
        else:
            upper_side[distance - 1] = incoming
    return (lower_side, upper_side)


def propagate_rows(local_tile, block_cols, trans_blocks):
    tile_height, tile_width = local_tile.shape
    blocks_here = block_cols.shape[0]
    block_size = trans_blocks.shape[2]
    total_blocks = blocks_here * lax.axis_size("rows")
    shards = -(-REACH // blocks_here)
    lower_side, upper_side = neighbor_strips(local_tile, shards)
    extended = jnp.concatenate(lower_side + [local_tile] + upper_side, axis=0)
    ext_blocks = extended.reshape(-1, block_size, tile_width)
    local_rows = jnp.arange(blocks_here, dtype=jnp.int32)
    first_block = lax.axis_index("rows") * blocks_here + local_rows
    offsets = (block_cols - first_block[:, None] + REACH) % total_blocks - REACH
    positions = shards * blocks_here + local_rows[:, None] + offsets
    result = jnp.zeros((blocks_here, block_size, tile_width), jnp.float32)
    for column_slot in range(block_cols.shape[1]):
        picked = jnp.take(ext_blocks, positions[:, column_slot], axis=0)
        result = result + jnp.einsum(
            "iab,ibw->iaw", trans_blocks[:, column_slot], picked, precision=lax.Precision.HIGHEST
        )
    return result.reshape(tile_height, tile_width)


def transpose_tile(local_tile):
    tile_height, tile_width = local_tile.shape
    col_count = lax.axis_size("cols")
    row_group = lax.axis_size("rows") // col_count
    quarter = tile_height // col_count
    section_one = lax.all_to_all(local_tile, "cols", split_axis=0, concat_axis=1, tiled=True)
    arrived = lax.all_to_all(
        lax.all_to_all(section_one, "rows", split_axis=1, concat_axis=0, tiled=True),
        "cols",
        split_axis=0,
        concat_axis=1,
        tiled=True,
    )
    pieces = arrived.reshape(row_group, quarter, col_count, tile_height)
    return jnp.transpose(pieces, (3, 0, 2, 1)).reshape(tile_height, tile_width)


def noise_tile(noise_pattern, noise_table, tile_height, tile_width):
    block_size = noise_table.shape[1]
    kinds = noise_table.shape[0]
    blocks_here = noise_pattern.shape[0]
    row_group = lax.axis_size("rows") // lax.axis_size("cols")
    row_index = lax.axis_index("rows")
    present = (row_index // row_group == lax.axis_index("cols")).astype(jnp.float32)
    symmetric = (noise_table + jnp.transpose(noise_table, (0, 2, 1))) * 0.5
    onehot = (noise_pattern[:, None] == jnp.arange(kinds, dtype=jnp.int32)[None, :]).astype(
        jnp.float32
    )
    picked = jnp.dot(
        onehot,
        symmetric.reshape(kinds, block_size * block_size),
        precision=lax.Precision.HIGHEST,
        preferred_element_type=jnp.float32,
    )
    picked = picked.reshape(blocks_here, block_size, block_size)
    identity = jnp.eye(blocks_here, dtype=jnp.float32)
    diagonal_tile = (picked[:, :, None, :] * identity[:, None, :, None]).reshape(
        tile_height, tile_height
    )
    start = row_index % row_group * tile_height
    placed = lax.dynamic_update_slice(
        jnp.zeros((tile_height, tile_width), jnp.float32), diagonal_tile, (jnp.int32(0), start)
    )
    return present * placed


def split(value):
    high = value.astype(jnp.bfloat16)
    return high, (value - high.astype(jnp.float32)).astype(jnp.bfloat16)


def product(left, right):
    left_high, left_low = left
    right_high, right_low = right
    dot = functools.partial(jnp.dot, preferred_element_type=jnp.float32)
    return dot(left_high, right_high) + (dot(left_high, right_low) + dot(left_low, right_high))


def square_kernel(
    size,
    cols_ref,
    pattern_ref,
    cov_ref,
    trans_ref,
    table_ref,
    out_ref,
    trans,
    table,
    own,
    rows_high,
    rows_low,
    turned_high,
    turned_low,
    tiles,
    sending,
    turned,
    pieces,
    noise,
    local_sem,
    tile_send,
    tile_recv,
    piece_send,
    piece_recv,
):
    group = lax.axis_index("groups")
    row = lax.axis_index("rows")
    col = lax.axis_index("cols")
    diagonal = row == col

    get_cov = pltpu.make_async_copy(cov_ref, own, local_sem.at[0])
    get_trans = pltpu.make_async_copy(trans_ref, trans, local_sem.at[1])
    get_table = pltpu.make_async_copy(table_ref, table, local_sem.at[2])
    get_cov.start()
    get_trans.start()
    get_table.start()

    barrier = pltpu.get_barrier_semaphore()

    def greet(to_row, to_col):
        pl.semaphore_signal(
            barrier, inc=1, device_id=(group, to_row, to_col), device_id_type=MESH
        )

    for step in range(1, size):
        greet((row + step) % size, col)
        greet(col, (row + step) % size)

    @pl.when(jnp.logical_not(diagonal))
    def _():
        greet(col, row)

    get_cov.wait()
    sending[...] = own[...].T
    get_trans.wait()
    for j in range(size):
        block = jnp.zeros(own.shape, jnp.float32)
        for k in range(trans.shape[1]):
            block = block + jnp.where(cols_ref[0, k] == j, trans[0, k], 0.0)
        high, low = split(block)
        rows_high[j] = high
        rows_low[j] = low
        high, low = split(block.T)
        turned_high[j] = high
        turned_low[j] = low
    get_table.wait()
    noise[...] = jnp.zeros(noise.shape, jnp.float32)

    @pl.when(diagonal)
    def _():
        kind = table[pattern_ref[0]]
        noise[...] = (kind + kind.T) * 0.5

    @pl.when(diagonal)
    def _():
        pl.semaphore_wait(barrier, 2 * (size - 1))

    @pl.when(jnp.logical_not(diagonal))
    def _():
        pl.semaphore_wait(barrier, 2 * size - 1)

    depth = own.shape[0] // CHUNKS

    def tile_copy(step, chunk):
        rows = pl.ds(chunk * depth, depth)
        return pltpu.make_async_remote_copy(
            src_ref=sending.at[rows],
            dst_ref=tiles.at[step - 1, rows],
            send_sem=tile_send.at[step - 1, chunk],
            recv_sem=tile_recv.at[step - 1, chunk],
            device_id=(group, (row + step) % size, col),
            device_id_type=MESH,
        )

    def piece_copy(step, chunk):
        rows = pl.ds(chunk * depth, depth)
        return pltpu.make_async_remote_copy(
            src_ref=turned.at[rows],
            dst_ref=pieces.at[col, rows],
            send_sem=piece_send.at[step, chunk],
            recv_sem=piece_recv.at[col, chunk],
            device_id=(group, (row + step) % size, row),
            device_id_type=MESH,
        )

    def arrival(source, chunk):
        rows = pl.ds(chunk * depth, depth)
        return pltpu.make_async_remote_copy(
            src_ref=turned.at[rows],
            dst_ref=pieces.at[source, rows],
            send_sem=piece_send.at[0, chunk],
            recv_sem=piece_recv.at[source, chunk],
            device_id=(group, col, source),
            device_id_type=MESH,
        )

    for chunk in range(CHUNKS):
        for step in range(1, size):
            tile_copy(step, chunk).start()

    for chunk in range(CHUNKS):
        rows = pl.ds(chunk * depth, depth)
        total = product(split(sending[rows]), (turned_high[row], turned_low[row]))
        for step in range(1, size):
            tile_copy(step, chunk).wait_recv()
            source = (row + size - step) % size
            total = total + product(
                split(tiles[step - 1, rows]), (turned_high[source], turned_low[source])
            )
        turned[rows] = total
        for step in range(1, size):
            piece_copy(step, chunk).start()

        @pl.when(jnp.logical_not(diagonal))
        def _():
            piece_copy(0, chunk).start()

    @pl.when(diagonal)
    def _():
        pieces[col] = turned[...]

    result = noise[...]
    for step in range(size):
        source = (col + step) % size
        for chunk in range(CHUNKS):
            if step == 0:

                @pl.when(jnp.logical_not(diagonal))
                def _():
                    arrival(source, chunk).wait_recv()
            else:
                arrival(source, chunk).wait_recv()
        result = result + product(
            (rows_high[source], rows_low[source]), split(pieces[source])
        )
    out_ref[...] = result

    for chunk in range(CHUNKS):
        for step in range(1, size):
            tile_copy(step, chunk).wait_send()
            piece_copy(step, chunk).wait_send()

        @pl.when(jnp.logical_not(diagonal))
        def _():
            piece_copy(0, chunk).wait_send()


def square_body(covariance, block_cols, trans_blocks, noise_pattern, noise_table):
    size = lax.axis_size("rows")
    tile = covariance.shape
    copies = pltpu.SemaphoreType.DMA
    return pl.pallas_call(
        functools.partial(square_kernel, size),
        out_shape=jax.ShapeDtypeStruct(tile, jnp.float32),
        in_specs=[
            pl.BlockSpec(memory_space=pltpu.SMEM),
            pl.BlockSpec(memory_space=pltpu.SMEM),
            pl.BlockSpec(memory_space=pl.ANY),
            pl.BlockSpec(memory_space=pl.ANY),
            pl.BlockSpec(memory_space=pl.ANY),
        ],
        out_specs=pl.BlockSpec(memory_space=pltpu.VMEM),
        scratch_shapes=[
            pltpu.VMEM(trans_blocks.shape, jnp.float32),
            pltpu.VMEM(noise_table.shape, jnp.float32),
            pltpu.VMEM(tile, jnp.float32),
            pltpu.VMEM((size, *tile), jnp.bfloat16),
            pltpu.VMEM((size, *tile), jnp.bfloat16),
            pltpu.VMEM((size, *tile), jnp.bfloat16),
            pltpu.VMEM((size, *tile), jnp.bfloat16),
            pltpu.VMEM((size - 1, *tile), jnp.float32),
            pltpu.VMEM(tile, jnp.float32),
            pltpu.VMEM(tile, jnp.float32),
            pltpu.VMEM((size, *tile), jnp.float32),
            pltpu.VMEM(tile, jnp.float32),
            copies((3,)),
            copies((size - 1, CHUNKS)),
            copies((size - 1, CHUNKS)),
            copies((size, CHUNKS)),
            copies((size, CHUNKS)),
        ],
        compiler_params=pltpu.CompilerParams(collective_id=0, has_side_effects=True),
    )(block_cols, noise_pattern, covariance, trans_blocks, noise_table)


def body(covariance, block_cols, trans_blocks, noise_pattern, noise_table):
    tile_height, tile_width = covariance.shape
    propagated = propagate_rows(covariance, block_cols, trans_blocks)
    carried = propagate_rows(transpose_tile(propagated), block_cols, trans_blocks)
    return carried + noise_tile(noise_pattern, noise_table, tile_height, tile_width)


def device_body(covariance, block_cols, trans_blocks, noise_pattern, noise_table):
    block = trans_blocks.shape[2]
    square = lax.axis_size("rows") == lax.axis_size("cols")
    chosen = square_body if square and covariance.shape == (block, block) else body
    return chosen(covariance, block_cols, trans_blocks, noise_pattern, noise_table)


def solution(mesh):
    placed = (
        P(("groups", "rows"), "cols"),
        P(("groups", "rows"), None),
        P(("groups", "rows"), None, None, None),
        P(("groups", "rows")),
        P(),
    )
    return jax.shard_map(
        device_body, mesh=mesh, in_specs=placed, out_specs=P(("groups", "rows"), "cols"), check_vma=False
    )
```
